512 devices in a mesh: dp: 16 (over z, core), enc: 32 (over y, x).
Axes of the slice: x: 4, y: 8, z: 8, core: 2. Of those that a mesh axis runs over, the one named last changes fastest.
Arguments:
- patches: bfloat16 [512, 128, 640], P(('dp', 'enc')), may hold values from -6 to 6
- lengths: int32 [512], P('dp'), may hold values from 32 to 128, as said below
- offsets: int32 [512], P('dp'), may hold values from 0 to 8064, as said below
- w_qkv: bfloat16 [640, 1920], P(None, 'enc')
- w_out: bfloat16 [640, 640], P(None, 'enc'), may hold values from -0.25 to 0.25
- d_embeds: bfloat16 [131072, 640], P(('dp', 'enc')), may hold values from -24 to 24
Outputs:
- embeds: bfloat16 [131072, 640], P(('dp', 'enc'))
- d_patches: bfloat16 [512, 128, 640], P(('dp', 'enc'))
- grad_qkv: float32 [640, 1920], P(None, 'enc')
- grad_out: float32 [640, 640], P(None, 'enc')
The draws below stay inside these ranges and needn't reach their ends.
Inputs may be any that keep to these rules, and one draw needn't show every extreme that they name: `lengths`: each group of 32 images holds one image of exactly 128 patches. Within a group the positions offsets[i] to offsets[i] + lengths[i] - 1 of different images never meet, and offsets[i] + 128 <= 8192.
All inputs are finite; a program needn't handle non-finite values.
Results may differ from the reference program's by a relative error of at most 0.02.
The reference program's roundings to bfloat16 on the way count: a program that leaves them out, or rounds other values in their place, can miss the bound.
Values may be sent and summed in bfloat16 or wider, within the bound.
No kernel may reach another device: no remote copies, remote signals or barrier semaphores. Data moves between devices by JAX's collectives and lax.ppermute only.
A program may use at most 64 MiB of HBM per device.

```python
import math
import jax
import jax.numpy as jnp
from jax import lax

D = 640
HEADS = 8
HEAD_DIM = 80
CAP = 128
SLOTS = 1
HEAD_COLS = 640
QKV_COLS = 1920
SEQ_ROWS = 256
GROUP_IMAGES = 32
IMAGES = 512
EMBED_ROWS = 131072
N_ENC = 32
DEVICES = 512


def layout(key):
    groups_all = IMAGES // GROUP_IMAGES
    first_key, second_key, third_key, fourth_key = jax.random.split(key, 4)
    patch_counts = jax.random.randint(first_key, (groups_all, GROUP_IMAGES), CAP // 4, CAP + 1)
    full_at = jax.random.randint(second_key, (groups_all, 1), 0, GROUP_IMAGES)
    column = jnp.arange(GROUP_IMAGES, dtype=jnp.int32)[None, :]
    patch_counts = jnp.where(column == full_at, CAP, patch_counts)
    text_gaps = jax.random.randint(third_key, (groups_all, GROUP_IMAGES), 0, CAP)
    placing = jax.vmap(lambda one_key: jax.random.permutation(one_key, GROUP_IMAGES))(jax.random.split(fourth_key, groups_all))
    span_rows = jnp.take_along_axis(patch_counts, placing, axis=1) + text_gaps
    starts = jnp.cumsum(span_rows, axis=1) - span_rows
    starts = jnp.where(column == GROUP_IMAGES - 1, N_ENC * SEQ_ROWS - CAP, starts)
    group_rows = jnp.broadcast_to(jnp.arange(groups_all, dtype=jnp.int32)[:, None], placing.shape)
    placed = jnp.zeros_like(patch_counts).at[group_rows, placing].set(starts)
    return (patch_counts.reshape(-1).astype(jnp.int32), placed.reshape(-1).astype(jnp.int32))


def draw_lengths(key, part):
    return layout(key)[0]


def draw_offsets(key, part):
    return layout(key)[1]


def draw_w_qkv(key, part):
    key = jax.random.fold_in(key, 7)
    law_key = jax.random.fold_in(key, 0)
    column = jnp.arange(QKV_COLS, dtype=jnp.int32)
    kind_of = column // HEAD_COLS
    base = jnp.where(kind_of < 2, 2.0, 1.0).astype(jnp.float32) / math.sqrt(D)
    noise = jax.random.normal(law_key, (D, QKV_COLS), jnp.float32)
    return (noise * base[None, :]).astype(jnp.bfloat16)


def with_spikes(drawn, stream_key, source, target, parts, factor):
    owner, partner = [(jnp.arange(drawn.shape[axis_at]) // (drawn.shape[axis_at] // parts)).reshape([-1 if axis == axis_at else 1 for axis in range(drawn.ndim)]) for axis_at in (source, target)]
    chosen = jax.random.permutation(stream_key, parts)[partner]
    strong = (owner == chosen) | (owner == (partner + parts // 2) % parts)
    return jnp.where(strong, factor * drawn, drawn)


def levels(key, shape, pieces, least, top_value):
    factor_of = 1.0
    for dim, shards_of in pieces:
        steps = jax.random.uniform(jax.random.fold_in(jax.random.fold_in(key, 6), dim), (shards_of,), jnp.float32, least / len(pieces), top_value / len(pieces))
        factor_of = factor_of * jnp.repeat(jnp.exp(steps), shape[dim] // shards_of).reshape((-1,) + (1,) * (len(shape) - 1 - dim))
    return factor_of


def bell_draw(rng, extent, scale, limit, pieces=(), kind=jnp.bfloat16):
    level = levels(rng, extent, pieces, -0.22, 0.18) if pieces else 1.0
    result = jax.random.normal(rng, extent, jnp.float32) * scale * level
    return jnp.minimum(jnp.maximum(result, -limit), limit).astype(kind)


def noise_with(stream_key, extent, scale, bound, cuts, heavy, kind=jnp.bfloat16):
    result = scale * jax.random.normal(stream_key, extent, jnp.float32)
    if cuts:
        result = result * levels(stream_key, extent, cuts, -0.22, 0.18)
    return jnp.clip(with_spikes(result, jax.random.fold_in(stream_key, 3), *heavy), -bound, bound).astype(kind)


def setup_inputs(seed: int = 0) -> dict:
    splits = jax.random.split(jax.random.key(seed), 7)
    return {
        "patches": bell_draw(splits[0], (IMAGES, CAP, D), 1.0, 6.0, ((0, 512),)),
        "lengths": draw_lengths(jax.random.fold_in(splits[6], 71), 0),
        "offsets": draw_offsets(jax.random.fold_in(splits[6], 71), 0),
        "w_qkv": draw_w_qkv(jax.random.fold_in(splits[6], 71), 0),
        "w_out": bell_draw(splits[4], (HEAD_COLS, D), HEAD_COLS ** -0.5, 0.25, ((1, 32),)),
        "d_embeds": noise_with(splits[5], (EMBED_ROWS, D), 1.0, 24.0, ((0, 512),), (0, 1, 128, 5.5)),
    }


def lowered(term):
    return lax.optimization_barrier(term.astype(jnp.bfloat16)).astype(jnp.float32)

def normalize(patch_block):
    values_f = patch_block.astype(jnp.float32)
    inverse = lax.rsqrt(lax.optimization_barrier(jnp.mean(values_f * values_f, axis=-1, keepdims=True)) + 1e-06)
    return (values_f, inverse, (values_f * inverse).astype(jnp.bfloat16))

def attention_weights(queries, keys_in, allowed):
    scores = jnp.einsum('gqhe,gkhe->ghqk', queries.astype(jnp.float32), keys_in.astype(jnp.float32)) * HEAD_DIM ** (-0.5)
    allowed = allowed[:, None]
    scores = jnp.where(allowed, scores, -1e+30)
    highest = lax.optimization_barrier(jnp.max(scores, axis=-1, keepdims=True))
    weights = jnp.where(allowed, jnp.exp(scores - highest), 0.0)
    return weights / lax.optimization_barrier(jnp.sum(weights, axis=-1, keepdims=True))

def reference(patches, lengths, offsets, w_qkv, w_out, d_embeds):
    owners = N_ENC
    row_count = SLOTS * CAP
    slot_iota = jnp.arange(CAP, dtype=jnp.int32)

    def device_step(running, inputs):
        qkv_running, out_running = running
        device_patches, own_lengths, own_offsets, device = inputs
        group_index = device // owners
        values_f, inverse, normed = normalize(device_patches)
        normed_rows = normed.reshape(row_count, D)
        projected = jnp.dot(normed_rows, w_qkv, preferred_element_type=jnp.float32).astype(jnp.bfloat16)
        projected = projected.reshape(SLOTS, CAP, 3, HEADS, HEAD_DIM)
        queries, keys_in, values_in = (projected[:, :, 0], projected[:, :, 1], projected[:, :, 2])
        present = slot_iota[None, :] < own_lengths[:, None]
        allowed = present[:, None, :]
        weights = attention_weights(queries, keys_in, allowed)
        weights_low = weights.astype(jnp.bfloat16)
        context = jnp.einsum('ghqk,gkhe->gqhe', weights_low.astype(jnp.float32), values_in.astype(jnp.float32)).astype(jnp.bfloat16)
        context = context.reshape(row_count, HEAD_COLS)
        layer_out = values_f + jnp.dot(context, w_out, preferred_element_type=jnp.float32).reshape(SLOTS, CAP, D)
        outgoing = jnp.where(present[:, :, None], layer_out, 0.0).astype(jnp.bfloat16)
        positions = own_offsets[:, None] + slot_iota[None, :]
        target = (group_index * owners + positions % owners) * SEQ_ROWS + positions // owners
        grad_rows = jnp.where(present[:, :, None], d_embeds[target], jnp.zeros((), jnp.bfloat16))
        grad_flat = grad_rows.reshape(row_count, D)
        d_context = jnp.dot(grad_flat, w_out.T, preferred_element_type=jnp.float32).astype(jnp.bfloat16)
        out_term = jnp.dot(context.T, grad_flat, preferred_element_type=jnp.float32)
        d_context4 = d_context.reshape(SLOTS, CAP, HEADS, HEAD_DIM).astype(jnp.float32)
        d_weights = jnp.einsum('gqhe,gkhe->ghqk', d_context4, values_in.astype(jnp.float32))
        d_values = jnp.einsum('ghqk,gqhe->gkhe', weights_low.astype(jnp.float32), d_context4)
        d_scores = (weights * (d_weights - lax.optimization_barrier(jnp.sum(d_weights * weights, axis=-1, keepdims=True))) * HEAD_DIM ** (-0.5)).astype(jnp.bfloat16)
        d_queries = jnp.einsum('ghqk,gkhe->gqhe', d_scores.astype(jnp.float32), keys_in.astype(jnp.float32))
        d_keys = jnp.einsum('ghqk,gqhe->gkhe', d_scores.astype(jnp.float32), queries.astype(jnp.float32))
        d_qkv = jnp.stack([d_queries, d_keys, d_values], axis=2).astype(jnp.bfloat16).reshape(row_count, QKV_COLS)
        qkv_term = jnp.dot(normed_rows.T, d_qkv, preferred_element_type=jnp.float32)
        d_normed = jnp.dot(d_qkv, w_qkv.T, preferred_element_type=jnp.float32).reshape(SLOTS, CAP, D)
        d_inputs = grad_rows.astype(jnp.float32) + inverse * (d_normed - values_f * inverse * inverse * lax.optimization_barrier(jnp.mean(d_normed * values_f, axis=-1, keepdims=True)))
        running = (qkv_running + lowered(qkv_term), out_running + lowered(out_term))
        return (running, (outgoing, target, d_inputs.astype(jnp.bfloat16)))
    start = (jnp.zeros((D, QKV_COLS), jnp.float32), jnp.zeros((HEAD_COLS, D), jnp.float32))
    inputs = (patches.reshape(DEVICES, SLOTS, CAP, D), lengths.reshape(DEVICES, SLOTS), offsets.reshape(DEVICES, SLOTS), jnp.arange(DEVICES, dtype=jnp.int32))
    (qkv_sum, out_sum), (sent_rows, targets, d_inputs) = lax.scan(device_step, start, inputs)
    embeds = jnp.zeros((EMBED_ROWS, D), jnp.bfloat16).at[targets.reshape(-1)].add(sent_rows.reshape(-1, D))
    factor = 1.0 / math.sqrt(IMAGES * CAP)
    return (embeds, d_inputs.reshape(IMAGES, CAP, D), qkv_sum * factor, out_sum * factor)
```

```python
import functools
import math

import jax
import jax.numpy as jnp
from jax import lax
from jax.experimental import pallas as pl
from jax.experimental.pallas import tpu as pltpu
from jax.sharding import Mesh, PartitionSpec as P

HEADS = 8
HEAD_DIM = 80
D = 640
CAP = 128
NX, NY, NZ = 4, 8, 8
OWNERS = NX * NY
QP, OP = 30, 10
PIECE = QP + OP
ROWS = NY * PIECE
W_EMB = CAP // OWNERS
EX = NY * W_EMB
EY = NX * W_EMB
SCALE = HEAD_DIM ** (-0.5)
BF = jnp.bfloat16
F32 = jnp.float32
VMEM_LIMIT = 56 * 1024 * 1024

PIECES = [(x, y) for x in range(NX) for y in range(NY)]


def dot(a, b, ca, cb):
    return lax.dot_general(a, b, (((ca,), (cb,)), ((), ())), preferred_element_type=F32)


def call(kernel, out_shape, scratch, *args, smem=1):
    specs = [pl.BlockSpec(memory_space=pltpu.SMEM)] * smem + [
        pl.BlockSpec(memory_space=pltpu.VMEM)
    ] * (len(args) - smem)
    return pl.pallas_call(
        kernel,
        out_shape=out_shape,
        in_specs=specs,
        out_specs=jax.tree.map(lambda _: pl.BlockSpec(memory_space=pltpu.VMEM), out_shape),
        scratch_shapes=scratch,
        compiler_params=pltpu.CompilerParams(vmem_limit_bytes=VMEM_LIMIT),
    )(*args)


def sds(shape, dtype=BF):
    return jax.ShapeDtypeStruct(shape, dtype)


def target_rows(offsets, owner, within):
    return ((offsets + ((owner - offsets) & (OWNERS - 1))) >> 5) + within


def pre_kernel(info, offs, d_embeds, wq, wo, send, fq, fo):
    core, owner = info[0], info[1]
    seq_rows = d_embeds.shape[0]
    shape = (CAP, seq_rows)
    within = lax.broadcasted_iota(jnp.int32, (CAP, 1), 0) & (W_EMB - 1)
    rows = target_rows(offs[...], owner, within)
    pick = (lax.broadcasted_iota(jnp.int32, shape, 1) == rows).astype(F32).astype(BF)
    fetched = dot(pick, d_embeds[...], 1, 0).astype(BF)
    fq[...] = wq[...].astype(F32)
    fo[...] = wo[...].astype(F32)
    first = core == 0
    half_q = jnp.where(first, fq[0:QP], fq[QP : 2 * QP])
    half_o = jnp.where(first, fo[0:OP], fo[OP : 2 * OP])
    fq[0:QP] = half_q
    fq[QP:PIECE] = half_o
    piece = fq[0:PIECE].astype(BF)
    for y in range(NY):
        send[y, 0:EY] = fetched[y * EY : (y + 1) * EY]
        send[y, EY : EY + PIECE] = piece


def normalize(patches):
    values_f = patches[...].astype(F32)
    inverse = lax.rsqrt(jnp.mean(values_f * values_f, axis=-1, keepdims=True) + 1e-06)
    return values_f, inverse, (values_f * inverse).astype(BF)


def fwd_kernel(
    info, patches, own, other, going, qkv_t, prob, ctx_t, pa, pb, qf, layer_t
):
    core, length, offset = info[0], info[2], info[3]
    first = core == 0
    values_f, _, normed = normalize(patches)
    for x in range(NX):
        block = slice(x * ROWS, (x + 1) * ROWS)
        pa[block] = dot(own[x, EX:], normed, 1, 1)
        pb[block] = dot(other[x, EX:], normed, 1, 1)
    for n, (x, y) in enumerate(PIECES):
        low, dest = n * PIECE, 2 * QP * (NX * y + x)
        mine, theirs = pa[low : low + QP], pb[low : low + QP]
        qf[dest : dest + QP] = jnp.where(first, mine, theirs)
        qf[dest + QP : dest + 2 * QP] = jnp.where(first, theirs, mine)
    qkv_t[...] = qf[...].astype(BF)
    allowed = lax.broadcasted_iota(jnp.int32, (CAP, CAP), 1) < length
    for h in range(HEADS):
        q, k, v = (
            qkv_t[pl.ds(part * D + h * HEAD_DIM, HEAD_DIM), :] for part in range(3)
        )
        scores = jnp.where(allowed, dot(q, k, 0, 0) * SCALE, -1e30)
        highest = jnp.max(scores, axis=-1, keepdims=True)
        weights = jnp.where(allowed, jnp.exp(scores - highest), 0.0)
        weights = weights / jnp.sum(weights, axis=-1, keepdims=True)
        prob[h] = weights
        ctx_t[pl.ds(h * HEAD_DIM, HEAD_DIM), :] = dot(v, weights.astype(BF), 1, 1).astype(BF)
    context = ctx_t[...]
    for x in range(NX):
        block = slice(x * ROWS, (x + 1) * ROWS)
        pa[block] = dot(own[x, EX:], context, 1, 0)
        pb[block] = dot(other[x, EX:], context, 1, 0)
    for n, (x, y) in enumerate(PIECES):
        low, dest = n * PIECE + QP, 2 * OP * (NX * y + x)
        mine, theirs = pa[low : low + OP], pb[low : low + OP]
        layer_t[dest : dest + OP] = jnp.where(first, mine, theirs)
        layer_t[dest + OP : dest + 2 * OP] = jnp.where(first, theirs, mine)
    layer_out = values_f + layer_t[...].T
    slot = lax.broadcasted_iota(jnp.int32, (CAP, 1), 0)
    outgoing = jnp.where(slot < length, layer_out, 0.0).astype(BF)
    row = lax.broadcasted_iota(jnp.int32, (CAP, CAP), 0)
    x, y, w = row >> 5, (row >> 2) & 7, row & 3
    source = w * OWNERS + ((NX * y + x - offset) & (OWNERS - 1))
    order = (lax.broadcasted_iota(jnp.int32, (CAP, CAP), 1) == source).astype(F32).astype(BF)
    going[...] = dot(order, outgoing, 1, 0).astype(BF)


def bwd_kernel(
    info, patches, own, other, qkv_t, prob, ctx_t, going,
    part_own, part_other, d_patches, grad_t, dq, la, lb,
):
    core, length, offset = info[0], info[2], info[3]
    first = core == 0
    values_f, inverse, normed = normalize(patches)
    came = jnp.concatenate([own[x, 0:EX] for x in range(NX)], axis=0)
    slot = lax.broadcasted_iota(jnp.int32, (CAP, CAP), 0)
    owner = (slot + offset) & (OWNERS - 1)
    source = (owner & 3) * EX + (owner >> 2) * W_EMB + (slot >> 5)
    column = lax.broadcasted_iota(jnp.int32, (CAP, CAP), 1)
    pick = ((column == source) & (slot < length)).astype(F32).astype(BF)
    grad_f = dot(pick, came, 1, 0)
    grad_t[...] = grad_f.T
    la[...] = jnp.zeros_like(la)
    lb[...] = jnp.zeros_like(lb)
    for n, (x, y) in enumerate(PIECES):
        low, src = n * PIECE + QP, 2 * OP * (NX * y + x)
        one, two = grad_t[src : src + OP], grad_t[src + OP : src + 2 * OP]
        la[low : low + OP, CAP:] = jnp.where(first, one, two)
        lb[low : low + OP, CAP:] = jnp.where(first, two, one)

    def back(ref, lanes):
        total = None
        for half, weights in ((la, own), (lb, other)):
            for x in range(NX):
                left = half[x * ROWS : (x + 1) * ROWS, lanes].T.astype(BF)
                term = dot(left, weights[x, EX:], 1, 0)
                total = term if total is None else total + term
        return total

    d_ctx_t = back(None, slice(CAP, 2 * CAP)).astype(BF).astype(F32).T.astype(BF)
    for h in range(HEADS):
        at = [pl.ds(part * D + h * HEAD_DIM, HEAD_DIM) for part in range(3)]
        q, k, v = (qkv_t[rows, :] for rows in at)
        dc = d_ctx_t[h * HEAD_DIM : (h + 1) * HEAD_DIM]
        weights = prob[h]
        d_prob = dot(dc, v, 0, 0)
        dq[at[2], :] = dot(dc, weights.astype(BF), 1, 0)
        inner = jnp.sum(d_prob * weights, axis=-1, keepdims=True)
        d_scores = (weights * (d_prob - inner) * SCALE).astype(BF)
        dq[at[0], :] = dot(k, d_scores, 1, 1)
        dq[at[1], :] = dot(q, d_scores, 1, 0)
    for n, (x, y) in enumerate(PIECES):
        low, src = n * PIECE, 2 * QP * (NX * y + x)
        one, two = dq[src : src + QP], dq[src + QP : src + 2 * QP]
        la[low : low + QP, 0:CAP] = jnp.where(first, one, two)
        lb[low : low + QP, 0:CAP] = jnp.where(first, two, one)
    context = ctx_t[...].astype(F32).T.astype(BF)
    right = jnp.concatenate([normed, context], axis=0)
    for x in range(NX):
        block = slice(x * ROWS, (x + 1) * ROWS)
        part_own[x, 0:EX] = going[x * EX : (x + 1) * EX]
        part_other[x, 0:EX] = jnp.zeros((EX, D), BF)
        part_own[x, EX:] = dot(la[block].astype(BF), right, 1, 0).astype(BF)
        part_other[x, EX:] = dot(lb[block].astype(BF), right, 1, 0).astype(BF)
    d_normed = back(None, slice(0, CAP))
    d_patches[...] = (
        grad_f
        + inverse
        * (
            d_normed
            - values_f * inverse * inverse * jnp.mean(d_normed * values_f, axis=-1, keepdims=True)
        )
    ).astype(BF)


def place_kernel(info, offs, came, embeds):
    owner = info[1]
    rows = jnp.concatenate([came[y, 0:EY] for y in range(NY)], axis=0)
    within = lax.broadcasted_iota(jnp.int32, (1, CAP), 1) & (W_EMB - 1)
    target = target_rows(offs[...], owner, within)
    shape = (embeds.shape[0], CAP)
    place = (lax.broadcasted_iota(jnp.int32, shape, 0) == target).astype(F32).astype(BF)
    embeds[...] = dot(place, rows, 1, 0).astype(BF)


def swap(a):
    return lax.ppermute(a, "core", [(0, 1), (1, 0)])


def exchange(a, axis):
    return lax.all_to_all(a, axis, split_axis=0, concat_axis=0, tiled=True)


def local(patches, lengths, offsets, w_qkv, w_out, d_embeds):
    core = lax.axis_index("core")
    owner = lax.axis_index("y") * NX + lax.axis_index("x")
    seq_rows = d_embeds.shape[0]
    info = jnp.stack([core, owner, lengths[owner], offsets[owner]]).astype(jnp.int32)
    offs = jnp.repeat(offsets, W_EMB)
    tokens = patches.reshape(CAP, D)

    send = call(
        pre_kernel,
        sds((NY, EY + PIECE, D)),
        [pltpu.VMEM((2 * QP, D), F32), pltpu.VMEM((2 * OP, D), F32)],
        info, offs.reshape(CAP, 1), d_embeds, w_qkv.T, w_out.T,
    )
    got = exchange(send, "y")
    rows = got[:, :EY].reshape(NY, NX, W_EMB, D).transpose(1, 0, 2, 3).reshape(NX, EX, D)
    shards = jnp.broadcast_to(got[:, EY:].reshape(1, ROWS, D), (NX, ROWS, D))
    own = exchange(jnp.concatenate([rows, shards], axis=1), "x")
    other = swap(own)

    pieces = NX * ROWS
    going, qkv_t, prob, ctx_t = call(
        fwd_kernel,
        (sds((CAP, D)), sds((3 * D, CAP)), sds((HEADS, CAP, CAP), F32), sds((D, CAP))),
        [
            pltpu.VMEM((pieces, CAP), F32),
            pltpu.VMEM((pieces, CAP), F32),
            pltpu.VMEM((3 * D, CAP), F32),
            pltpu.VMEM((D, CAP), F32),
        ],
        info, tokens, own, other,
    )
    part_own, part_other, d_patches = call(
        bwd_kernel,
        (sds((NX, EX + ROWS, D)), sds((NX, EX + ROWS, D)), sds((CAP, D))),
        [
            pltpu.VMEM((D, CAP), F32),
            pltpu.VMEM((3 * D, CAP), F32),
            pltpu.VMEM((pieces, 2 * CAP), F32),
            pltpu.VMEM((pieces, 2 * CAP), F32),
        ],
        info, tokens, own, other, qkv_t, prob, ctx_t, going,
    )

    pair = (part_own.astype(F32) + swap(part_other).astype(F32)).astype(BF)
    got = exchange(pair, "x")
    rows = got[:, :EX].reshape(NX, NY, W_EMB, D).transpose(1, 0, 2, 3).reshape(NY, EY, D)
    total = jnp.sum(got[:, EX:].astype(F32), axis=0).astype(BF).reshape(NY, PIECE, D)
    got = exchange(jnp.concatenate([rows, total], axis=1), "y")
    embeds = call(
        place_kernel, sds((seq_rows, D)), [], info, offs.reshape(1, CAP), got
    )
    total = jnp.sum(got[:, EY:].astype(F32), axis=0).astype(BF)
    got = exchange(jnp.broadcast_to(total[None], (NZ, PIECE, D)), "z")
    factor = 1.0 / math.sqrt(CAP * OWNERS * 2 * NZ)
    mine = jnp.sum(got.astype(F32), axis=0) * factor
    theirs = swap(mine)
    low, high = jnp.where(core == 0, mine, theirs), jnp.where(core == 0, theirs, mine)
    grad_qkv = jnp.concatenate([low[:QP], high[:QP]], axis=0).T
    grad_out = jnp.concatenate([low[QP:], high[QP:]], axis=0).T
    return embeds, d_patches.reshape(patches.shape), grad_qkv, grad_out


def solution(mesh):
    axes = Mesh(mesh.devices.reshape(NZ, 2, NY, NX), ("z", "core", "y", "x"))
    group, plane = ("z", "core"), ("y", "x")
    return jax.shard_map(
        local,
        mesh=axes,
        in_specs=(
            P(group + plane, None, None),
            P(group),
            P(group),
            P(None, plane),
            P(None, plane),
            P(group + plane, None),
        ),
        out_specs=(
            P(group + plane, None),
            P(group + plane, None, None),
            P(None, plane),
            P(None, plane),
        ),
        check_vma=False,
    )
```

```python
import math

import jax
import jax.numpy as jnp
from jax import lax
from jax.experimental import pallas as pl
from jax.experimental.pallas import tpu as pltpu
from jax.sharding import Mesh, PartitionSpec as P

HEADS = 8
HEAD_DIM = 80
D = 640
CAP = 128
NX, NY, NZ = 4, 8, 8
OWNERS = NX * NY
QP, OP = 30, 10
PIECE = QP + OP
W_EMB = CAP // OWNERS
EX = NY * W_EMB
EY = NX * W_EMB
SCALE = HEAD_DIM ** (-0.5)
BF = jnp.bfloat16
F32 = jnp.float32
VMEM_LIMIT = 20 * 1024 * 1024
TEAM = 2 * NX
QB, OB = NY * QP, NY * OP
LB = D // CAP


def dot(a, b, ca, cb):
    return lax.dot_general(a, b, (((ca,), (cb,)), ((), ())), preferred_element_type=F32)


def call(kernel, out_shape, scratch, *args, smem=1, space=pltpu.VMEM, limit=VMEM_LIMIT):
    specs = [pl.BlockSpec(memory_space=pltpu.SMEM)] * smem + [
        pl.BlockSpec(memory_space=space)
    ] * (len(args) - smem)
    return pl.pallas_call(
        kernel,
        out_shape=out_shape,
        in_specs=specs,
        out_specs=jax.tree.map(lambda _: pl.BlockSpec(memory_space=pltpu.VMEM), out_shape),
        scratch_shapes=scratch,
        compiler_params=pltpu.CompilerParams(vmem_limit_bytes=limit),
    )(*args)


def sds(shape, dtype=BF):
    return jax.ShapeDtypeStruct(shape, dtype)


def here():
    return lax.axis_index("core"), lax.axis_index("y") * NX + lax.axis_index("x")


def target_rows(offsets):
    owner = here()[1]
    lane = lax.broadcasted_iota(jnp.int32, (1, CAP), 1)
    offset = jnp.zeros((1, CAP), jnp.int32)
    for image in range(OWNERS):
        offset = jnp.where(lane >> 2 == image, offsets[image], offset)
    return ((offset + ((owner - offset) & (OWNERS - 1))) >> 5) + (lane & (W_EMB - 1))


def one_hot(hit):
    return hit.astype(F32).astype(BF)


def reorder(rows, source):
    row = lax.broadcasted_iota(jnp.int32, (CAP, CAP), 0)
    column = lax.broadcasted_iota(jnp.int32, (CAP, CAP), 1)
    return dot(one_hot(column == source(row)), rows, 1, 0).astype(BF)


def put_rows(ref, first, rows):
    core = here()[0]
    for x in range(NX):
        for lane in range(LB):
            part = rows[x * EX : (x + 1) * EX, lane * CAP : (lane + 1) * CAP]
            ref[core * NX + x, first + lane * EX : first + (lane + 1) * EX] = part
        ref[(1 - core) * NX + x, first : first + LB * EX] = jnp.zeros((LB * EX, CAP), BF)


def get_rows(ref, first):
    core = here()[0]
    parts = []
    for x in range(NX):
        lanes = [
            ref[core * NX + x, first + lane * EX : first + (lane + 1) * EX] for lane in range(LB)
        ]
        parts.append(jnp.concatenate(lanes, axis=1))
    return jnp.concatenate(parts, axis=0)


def blocks():
    for core in range(2):
        for x in range(NX):
            for y in range(NY):
                yield core * NX + x, y, 2 * (NX * y + x) + core


def pre_kernel(offsets, *refs):
    sources, send, targets, sems, fq, fo = refs[:3], refs[3], refs[4:7], refs[7], *refs[8:]
    copies = [
        pltpu.make_async_copy(source, target, sems.at[n])
        for n, (source, target) in enumerate(zip(sources, targets, strict=True))
    ]
    for copy in copies:
        copy.start()
    for copy in copies:
        copy.wait()
    d_embeds, wq, wo = targets
    first = here()[0] == 0
    seq_rows = d_embeds.shape[0]
    row = lax.broadcasted_iota(jnp.int32, (seq_rows, CAP), 0)
    pick = one_hot(row == target_rows(offsets))
    fetched = dot(pick, d_embeds[...], 0, 0).astype(BF)
    fq[...] = wq[...].astype(F32)
    fo[...] = wo[...].astype(F32)
    half_q = jnp.where(first, fq[0:QP], fq[QP : 2 * QP])
    half_o = jnp.where(first, fo[0:OP], fo[OP : 2 * OP])
    fq[0:QP] = half_q
    fq[QP:PIECE] = half_o
    piece = fq[0:PIECE].astype(BF)
    for y in range(NY):
        send[y, 0:EY] = fetched[y * EY : (y + 1) * EY]
        send[y, EY : EY + PIECE] = piece


def normalize(patches):
    values_f = patches.astype(F32)
    inverse = lax.rsqrt(jnp.mean(values_f * values_f, axis=-1, keepdims=True) + 1e-06)
    return values_f, inverse, (values_f * inverse).astype(BF)


def qkv_kernel(mine, theirs, got, send, w_block, out_block, normed, tmp, fq, fo):
    core = here()[0]
    for y in range(NY):
        tmp[...] = got[y, EY : EY + PIECE].astype(F32)
        fq[y * QP : (y + 1) * QP] = tmp[0:QP]
        fo[y * OP : (y + 1) * OP] = tmp[QP:PIECE]
    weights = fq[...].astype(BF)
    w_block[...] = weights
    out_block[...] = fo[...].astype(BF)
    for side, patches in ((core, mine), (1 - core, theirs)):
        for x in range(NX):
            member = side * NX + x
            low = normalize(patches[x * CAP : (x + 1) * CAP])[2]
            normed[member] = low
            send[member, 0:QB] = dot(weights, low, 1, 1).astype(BF)
    rows = jnp.concatenate([got[y, 0:EY] for y in range(NY)], axis=0)
    rows = reorder(rows, lambda r: ((r >> 2) & 7) * EY + (r >> 5) * W_EMB + (r & 3))
    put_rows(send, QB, rows)


def fwd_kernel(lengths, got, qkv_t, prob, ctx_t, context, pa, qf):
    length = lengths[here()[1]]
    for member in range(TEAM):
        pa[member * QB : (member + 1) * QB] = got[member, 0:QB].astype(F32)
    for member, y, half in blocks():
        low = member * QB + y * QP
        qf[half * QP : (half + 1) * QP] = pa[low : low + QP]
    qkv_t[...] = qf[...].astype(BF)
    allowed = lax.broadcasted_iota(jnp.int32, (CAP, CAP), 1) < length
    for h in range(HEADS):
        q, k, v = (
            qkv_t[part * D + h * HEAD_DIM : part * D + (h + 1) * HEAD_DIM] for part in range(3)
        )
        scores = jnp.where(allowed, dot(q, k, 0, 0) * SCALE, -1e30)
        highest = jnp.max(scores, axis=-1, keepdims=True)
        weights = jnp.where(allowed, jnp.exp(scores - highest), 0.0)
        weights = weights / jnp.sum(weights, axis=-1, keepdims=True)
        prob[h] = weights
        ctx_t[h * HEAD_DIM : (h + 1) * HEAD_DIM] = dot(v, weights.astype(BF), 1, 1).astype(BF)
    context[...] = ctx_t[...].astype(F32).T.astype(BF)


def bwd_kernel(
    lengths, offsets, patches, got, qkv_t, prob, ctx_t, context, out_mine, out_theirs,
    send, grad, gt, gp, lt, oa, dq, dp,
):
    core, me = here()
    x_here = lax.axis_index("x")
    length, offset = lengths[me], offsets[me]
    came = get_rows(got, QB)
    slot = lax.broadcasted_iota(jnp.int32, (CAP, CAP), 0)
    owner = (slot + offset) & (OWNERS - 1)
    source = (owner & 3) * EX + (owner >> 2) * W_EMB + (slot >> 5)
    column = lax.broadcasted_iota(jnp.int32, (CAP, CAP), 1)
    grad_f = dot(one_hot((column == source) & (slot < length)), came, 1, 0)
    grad[...] = grad_f.astype(BF)
    gt[...] = grad_f.T
    for member, y, half in blocks():
        gp[member, y * OP : (y + 1) * OP] = gt[half * OP : (half + 1) * OP]
    out_blocks = [
        (side * NX + ((x_here - step) & (NX - 1)), ref[step * OB : (step + 1) * OB])
        for side, ref in ((core, out_mine), (1 - core, out_theirs))
        for step in range(NX)
    ]
    d_ctx = None
    for member, rows in out_blocks:
        term = dot(gp[member].T.astype(BF), rows, 1, 0)
        d_ctx = term if d_ctx is None else d_ctx + term
    d_ctx_t = d_ctx.astype(BF).astype(F32).T.astype(BF)
    for h in range(HEADS):
        at = [slice(part * D + h * HEAD_DIM, part * D + (h + 1) * HEAD_DIM) for part in range(3)]
        q, k, v = (qkv_t[rows] for rows in at)
        dc = d_ctx_t[h * HEAD_DIM : (h + 1) * HEAD_DIM]
        weights = prob[h]
        d_prob = dot(dc, v, 0, 0)
        dq[at[2]] = dot(dc, weights.astype(BF), 1, 0)
        inner = jnp.sum(d_prob * weights, axis=-1, keepdims=True)
        d_scores = (weights * (d_prob - inner) * SCALE).astype(BF)
        dq[at[0]] = dot(k, d_scores, 1, 1)
        dq[at[1]] = dot(q, d_scores, 1, 0)
    for member, y, half in blocks():
        low = member * QB + y * QP
        dp[low : low + QP] = dq[half * QP : (half + 1) * QP]
    for member in range(TEAM):
        send[member, 0:QB] = dp[member * QB : (member + 1) * QB].astype(BF)
        rows = gp[member].astype(BF)
        part = dot(rows, context[...], 1, 0).astype(BF)
        for lane in range(LB):
            low = QB + lane * OB
            send[member, low : low + OB] = part[:, lane * CAP : (lane + 1) * CAP]
    for member, rows in out_blocks:
        oa[member] = dot(rows, ctx_t[...], 1, 0)
    for member, y, half in blocks():
        lt[half * OP : (half + 1) * OP] = oa[member, y * OP : (y + 1) * OP]
    layer_out = patches[...].astype(F32) + lt[...].T
    token = lax.broadcasted_iota(jnp.int32, (CAP, 1), 0)
    outgoing = jnp.where(token < length, layer_out, 0.0).astype(BF)
    going = reorder(
        outgoing,
        lambda r: (r & 3) * OWNERS + ((NX * ((r >> 2) & 7) + (r >> 5) - offset) & (OWNERS - 1)),
    )
    put_rows(send, QB + LB * OB, going)


def grads_kernel(got, normed, send, fq, fo, tmp):
    total = None
    for member in range(TEAM):
        term = dot(got[member, 0:QB], normed[member], 1, 0)
        total = term if total is None else total + term
    fq[...] = total
    for lane in range(LB):
        low = QB + lane * OB
        total = got[0, low : low + OB].astype(F32)
        for member in range(1, TEAM):
            total += got[member, low : low + OB].astype(F32)
        fo[:, lane * CAP : (lane + 1) * CAP] = total
    rows = get_rows(got, QB + LB * OB)
    rows = reorder(rows, lambda r: ((r >> 2) & 3) * EX + (r >> 4) * W_EMB + (r & 3))
    for y in range(NY):
        tmp[0:QP] = fq[y * QP : (y + 1) * QP]
        tmp[QP:PIECE] = fo[y * OP : (y + 1) * OP]
        send[y, 0:EY] = rows[y * EY : (y + 1) * EY]
        send[y, EY : EY + PIECE] = tmp[...].astype(BF)


def terms_kernel(got, weights, mine, theirs):
    core = here()[0]
    for side, out in ((core, mine), (1 - core, theirs)):
        for x in range(NX):
            out[x] = dot(got[side * NX + x, 0:QB], weights[...], 0, 0).astype(BF)


def pair_kernel(mine, theirs, own, *others):
    x = lax.axis_index("x")
    for step, out in enumerate((own, *others)):
        image = (x + step) & (NX - 1)
        out[...] = (mine[image].astype(F32) + theirs[image].astype(F32)).astype(BF)


def patches_kernel(patches, grad, *refs):
    *terms, d_patches = refs
    d_normed = terms[0][...].astype(F32)
    for term in terms[1:]:
        d_normed += term[...].astype(F32)
    values_f, inverse, _ = normalize(patches[...])
    mean = jnp.mean(d_normed * values_f, axis=-1, keepdims=True)
    d_inputs = inverse * (d_normed - values_f * inverse * inverse * mean)
    d_patches[...] = (grad[...].astype(F32) + d_inputs).astype(BF)


def place_kernel(offsets, came, embeds):
    rows = jnp.concatenate([came[y, 0:EY] for y in range(NY)], axis=0)
    row = lax.broadcasted_iota(jnp.int32, (embeds.shape[0], CAP), 0)
    embeds[...] = dot(one_hot(row == target_rows(offsets)), rows, 1, 0).astype(BF)


def to_right(a, step):
    return lax.ppermute(a, "x", [(x, (x + step) % NX) for x in range(NX)])


def swap(a):
    return lax.ppermute(a, "core", [(0, 1), (1, 0)])


def together(*arrays):
    return lax.optimization_barrier(arrays)


def exchange(a, axis):
    return lax.all_to_all(a, axis, split_axis=0, concat_axis=0, tiled=True)


def gather(a, axis):
    return lax.all_gather(a, axis, axis=0, tiled=True)


def local(patches, lengths, offsets, w_qkv, w_out, d_embeds):
    core = lax.axis_index("core")
    seq_rows = d_embeds.shape[0]
    tokens = patches.reshape(CAP, D)
    team = ("core", "x")
    scratch = pltpu.VMEM

    send = call(
        pre_kernel,
        sds((NY, EY + PIECE, D)),
        [
            scratch(d_embeds.shape, BF),
            scratch((2 * QP, D), BF),
            scratch((2 * OP, D), BF),
            pltpu.SemaphoreType.DMA((3,)),
            scratch((2 * QP, D), F32),
            scratch((2 * OP, D), F32),
        ],
        offsets, d_embeds, w_qkv.T, w_out.T, space=pltpu.HBM, limit=None,
    )
    got = exchange(send, "y")
    mine = gather(tokens, "x")
    theirs = swap(mine)
    send, w_block, out_block, normed = call(
        qkv_kernel,
        (sds((TEAM, QB + LB * EX, CAP)), sds((QB, D)), sds((OB, D)), sds((TEAM, CAP, D))),
        [scratch((PIECE, D), F32), scratch((QB, D), F32), scratch((OB, D), F32)],
        mine, theirs, got, smem=0,
    )
    got, *near = together(
        exchange(send, team), *[to_right(out_block, step) for step in range(1, NX)]
    )
    out_mine = jnp.concatenate([out_block, *near], axis=0)
    out_theirs = swap(out_mine)
    qkv_t, prob, ctx_t, context = call(
        fwd_kernel,
        (sds((3 * D, CAP)), sds((HEADS, CAP, CAP), F32), sds((D, CAP)), sds((CAP, D))),
        [scratch((3 * D, CAP), F32), scratch((3 * D, CAP), F32)],
        lengths, got,
    )
    send, grad = call(
        bwd_kernel,
        (sds((TEAM, QB + LB * (OB + EX), CAP)), sds((CAP, D))),
        [
            scratch((D, CAP), F32),
            scratch((TEAM, OB, CAP), F32),
            scratch((D, CAP), F32),
            scratch((TEAM, OB, CAP), F32),
            scratch((3 * D, CAP), F32),
            scratch((3 * D, CAP), F32),
        ],
        lengths, offsets, tokens, got, qkv_t, prob, ctx_t, context, out_mine, out_theirs,
        smem=2,
    )
    got = exchange(send, team)
    send = call(
        grads_kernel,
        sds((NY, EY + PIECE, D)),
        [scratch((QB, D), F32), scratch((OB, D), F32), scratch((PIECE, D), F32)],
        got, normed, smem=0,
    )
    send, got = together(send, got)
    term, other = call(
        terms_kernel,
        (sds((NX, CAP, D)), sds((NX, CAP, D))),
        [], got, w_block, smem=0,
    )
    got = exchange(send, "y")
    own, *others = call(
        pair_kernel, (sds((CAP, D)),) * NX, [], term, swap(other), smem=0
    )
    right, across, left = others
    got, right, left, across = together(got, to_right(right, 1), to_right(left, NX - 1), across)
    terms = (own, right, left, to_right(across, 2))
    embeds = call(place_kernel, sds((seq_rows, D)), [], offsets, got)
    total = jnp.sum(got[:, EY:].astype(F32), axis=0).astype(BF)
    got = exchange(jnp.broadcast_to(total[None], (NZ, PIECE, D)), "z")
    d_patches = call(
        patches_kernel, sds((CAP, D)), [],
        tokens, grad, *terms, smem=0,
    )
    got, d_patches, embeds = together(got, d_patches, embeds)
    factor = 1.0 / math.sqrt(CAP * OWNERS * 2 * NZ)
    own = jnp.sum(got.astype(F32), axis=0) * factor
    other = swap(own)
    low, high = jnp.where(core == 0, own, other), jnp.where(core == 0, other, own)
    grad_qkv = jnp.concatenate([low[:QP], high[:QP]], axis=0).T
    grad_out = jnp.concatenate([low[QP:], high[QP:]], axis=0).T
    return embeds, d_patches.reshape(patches.shape), grad_qkv, grad_out


def solution(mesh):
    axes = Mesh(mesh.devices.reshape(NZ, 2, NY, NX), ("z", "core", "y", "x"))
    group, plane = ("z", "core"), ("y", "x")
    return jax.shard_map(
        local,
        mesh=axes,
        in_specs=(
            P(group + plane, None, None),
            P(group),
            P(group),
            P(None, plane),
            P(None, plane),
            P(group + plane, None),
        ),
        out_specs=(
            P(group + plane, None),
            P(group + plane, None, None),
            P(None, plane),
            P(None, plane),
        ),
        check_vma=False,
    )
```

```python
import math

import jax
import jax.numpy as jnp
from jax import lax
from jax.experimental import pallas as pl
from jax.experimental.pallas import tpu as pltpu
from jax.sharding import Mesh, PartitionSpec as P

HEADS = 8
HEAD_DIM = 80
D = 640
CAP = 128
NX, NY, NZ = 4, 8, 8
OWNERS = NX * NY
QP, OP = 30, 10
PIECE = QP + OP
W_EMB = CAP // OWNERS
EX = NY * W_EMB
EY = NX * W_EMB
SCALE = HEAD_DIM ** (-0.5)
BF = jnp.bfloat16
F32 = jnp.float32
VMEM_LIMIT = 20 * 1024 * 1024
TEAM = 2 * NX
QB, OB = NY * QP, NY * OP
LB = D // CAP


def dot(a, b, ca, cb):
    return lax.dot_general(a, b, (((ca,), (cb,)), ((), ())), preferred_element_type=F32)


def call(kernel, out_shape, scratch, *args, smem=1, space=pltpu.VMEM, limit=VMEM_LIMIT):
    specs = [pl.BlockSpec(memory_space=pltpu.SMEM)] * smem + [
        pl.BlockSpec(memory_space=space)
    ] * (len(args) - smem)
    return pl.pallas_call(
        kernel,
        out_shape=out_shape,
        in_specs=specs,
        out_specs=jax.tree.map(lambda _: pl.BlockSpec(memory_space=pltpu.VMEM), out_shape),
        scratch_shapes=scratch,
        compiler_params=pltpu.CompilerParams(vmem_limit_bytes=limit),
    )(*args)


def sds(shape, dtype=BF):
    return jax.ShapeDtypeStruct(shape, dtype)


def here():
    return lax.axis_index("core"), lax.axis_index("y") * NX + lax.axis_index("x")


def target_rows(offsets):
    owner = here()[1]
    lane = lax.broadcasted_iota(jnp.int32, (1, CAP), 1)
    offset = jnp.zeros((1, CAP), jnp.int32)
    for image in range(OWNERS):
        offset = jnp.where(lane >> 2 == image, offsets[image], offset)
    return ((offset + ((owner - offset) & (OWNERS - 1))) >> 5) + (lane & (W_EMB - 1))


def one_hot(hit):
    return hit.astype(F32).astype(BF)


def reorder(rows, source):
    row = lax.broadcasted_iota(jnp.int32, (CAP, CAP), 0)
    column = lax.broadcasted_iota(jnp.int32, (CAP, CAP), 1)
    return dot(one_hot(column == source(row)), rows, 1, 0).astype(BF)


def put_rows(ref, first, rows):
    core = here()[0]
    for x in range(NX):
        for lane in range(LB):
            part = rows[x * EX : (x + 1) * EX, lane * CAP : (lane + 1) * CAP]
            ref[core * NX + x, first + lane * EX : first + (lane + 1) * EX] = part
        ref[(1 - core) * NX + x, first : first + LB * EX] = jnp.zeros((LB * EX, CAP), BF)


def get_rows(ref, first):
    core = here()[0]
    parts = []
    for x in range(NX):
        lanes = [
            ref[core * NX + x, first + lane * EX : first + (lane + 1) * EX] for lane in range(LB)
        ]
        parts.append(jnp.concatenate(lanes, axis=1))
    return jnp.concatenate(parts, axis=0)


def blocks():
    for core in range(2):
        for x in range(NX):
            for y in range(NY):
                yield core * NX + x, y, 2 * (NX * y + x) + core


def pre_kernel(offsets, *refs):
    sources, send, targets, sems, fq, fo = refs[:3], refs[3], refs[4:7], refs[7], *refs[8:]
    copies = [
        pltpu.make_async_copy(source, target, sems.at[n])
        for n, (source, target) in enumerate(zip(sources, targets, strict=True))
    ]
    for copy in copies:
        copy.start()
    d_embeds, wq, wo = targets
    first = here()[0] == 0
    seq_rows = d_embeds.shape[0]
    row = lax.broadcasted_iota(jnp.int32, (seq_rows, CAP), 0)
    pick = one_hot(row == target_rows(offsets))
    for copy in copies:
        copy.wait()
    fetched = dot(pick, d_embeds[...], 0, 0).astype(BF)
    fq[...] = wq[...].astype(F32)
    fo[...] = wo[...].astype(F32)
    half_q = jnp.where(first, fq[0:QP], fq[QP : 2 * QP])
    half_o = jnp.where(first, fo[0:OP], fo[OP : 2 * OP])
    fq[0:QP] = half_q
    fq[QP:PIECE] = half_o
    piece = fq[0:PIECE].astype(BF)
    for y in range(NY):
        send[y, 0:EY] = fetched[y * EY : (y + 1) * EY]
        send[y, EY : EY + PIECE] = piece


def normalize(patches):
    values_f = patches.astype(F32)
    inverse = lax.rsqrt(jnp.mean(values_f * values_f, axis=-1, keepdims=True) + 1e-06)
    return values_f, inverse, (values_f * inverse).astype(BF)


def qkv_kernel(mine, theirs, got, send, w_block, out_block, normed, tmp, fq, fo):
    core = here()[0]
    for y in range(NY):
        tmp[...] = got[y, EY : EY + PIECE].astype(F32)
        fq[y * QP : (y + 1) * QP] = tmp[0:QP]
        fo[y * OP : (y + 1) * OP] = tmp[QP:PIECE]
    weights = fq[...].astype(BF)
    w_block[...] = weights
    out_block[...] = fo[...].astype(BF)
    for side, patches in ((core, mine), (1 - core, theirs)):
        for x in range(NX):
            member = side * NX + x
            low = normalize(patches[x * CAP : (x + 1) * CAP])[2]
            normed[member] = low
            send[member, 0:QB] = dot(weights, low, 1, 1).astype(BF)
    rows = jnp.concatenate([got[y, 0:EY] for y in range(NY)], axis=0)
    rows = reorder(rows, lambda r: ((r >> 2) & 7) * EY + (r >> 5) * W_EMB + (r & 3))
    put_rows(send, QB, rows)


def fwd_kernel(lengths, got, qkv_t, prob, ctx_t, context, pa, qf):
    length = lengths[here()[1]]
    for member in range(TEAM):
        pa[member * QB : (member + 1) * QB] = got[member, 0:QB].astype(F32)
    for member, y, half in blocks():
        low = member * QB + y * QP
        qf[half * QP : (half + 1) * QP] = pa[low : low + QP]
    qkv_t[...] = qf[...].astype(BF)
    allowed = lax.broadcasted_iota(jnp.int32, (CAP, CAP), 1) < length
    for h in range(HEADS):
        q, k, v = (
            qkv_t[part * D + h * HEAD_DIM : part * D + (h + 1) * HEAD_DIM] for part in range(3)
        )
        scores = jnp.where(allowed, dot(q, k, 0, 0) * SCALE, -1e30)
        highest = jnp.max(scores, axis=-1, keepdims=True)
        weights = jnp.where(allowed, jnp.exp(scores - highest), 0.0)
        weights = weights / jnp.sum(weights, axis=-1, keepdims=True)
        prob[h] = weights
        ctx_t[h * HEAD_DIM : (h + 1) * HEAD_DIM] = dot(v, weights.astype(BF), 1, 1).astype(BF)
    context[...] = ctx_t[...].astype(F32).T.astype(BF)


def out_blocks(core, x_here, mine, theirs):
    for side, ref in ((core, mine), (1 - core, theirs)):
        for step in range(NX):
            member = side * NX + ((x_here - step) & (NX - 1))
            yield member, ref[step * OB : (step + 1) * OB]


def bwd_kernel(
    lengths, offsets, got, qkv_t, prob, context, out_mine, out_theirs, send,
    grad, gt, gp, dq, dp,
):
    core, me = here()
    x_here = lax.axis_index("x")
    length, offset = lengths[me], offsets[me]
    came = get_rows(got, QB)
    slot = lax.broadcasted_iota(jnp.int32, (CAP, CAP), 0)
    owner = (slot + offset) & (OWNERS - 1)
    source = (owner & 3) * EX + (owner >> 2) * W_EMB + (slot >> 5)
    column = lax.broadcasted_iota(jnp.int32, (CAP, CAP), 1)
    grad_f = dot(one_hot((column == source) & (slot < length)), came, 1, 0)
    grad[...] = grad_f.astype(BF)
    gt[...] = grad_f.T
    for member, y, half in blocks():
        gp[member, y * OP : (y + 1) * OP] = gt[half * OP : (half + 1) * OP]
    d_ctx = None
    for member, rows in out_blocks(core, x_here, out_mine, out_theirs):
        term = dot(gp[member].T.astype(BF), rows, 1, 0)
        d_ctx = term if d_ctx is None else d_ctx + term
    d_ctx_t = d_ctx.astype(BF).astype(F32).T.astype(BF)
    for h in range(HEADS):
        at = [slice(part * D + h * HEAD_DIM, part * D + (h + 1) * HEAD_DIM) for part in range(3)]
        q, k, v = (qkv_t[rows] for rows in at)
        dc = d_ctx_t[h * HEAD_DIM : (h + 1) * HEAD_DIM]
        weights = prob[h]
        d_prob = dot(dc, v, 0, 0)
        dq[at[2]] = dot(dc, weights.astype(BF), 1, 0)
        inner = jnp.sum(d_prob * weights, axis=-1, keepdims=True)
        d_scores = (weights * (d_prob - inner) * SCALE).astype(BF)
        dq[at[0]] = dot(k, d_scores, 1, 1)
        dq[at[1]] = dot(q, d_scores, 1, 0)
    for member, y, half in blocks():
        low = member * QB + y * QP
        dp[low : low + QP] = dq[half * QP : (half + 1) * QP]
    for member in range(TEAM):
        send[member, 0:QB] = dp[member * QB : (member + 1) * QB].astype(BF)
        rows = gp[member].astype(BF)
        part = dot(rows, context[...], 1, 0).astype(BF)
        for lane in range(LB):
            low = QB + lane * OB
            send[member, low : low + OB] = part[:, lane * CAP : (lane + 1) * CAP]


def out_kernel(lengths, offsets, patches, ctx_t, out_mine, out_theirs, *refs):
    along, (lt, oa, rows_x) = refs[:NX], refs[NX:]
    core, me = here()
    x_here = lax.axis_index("x")
    length, offset = lengths[me], offsets[me]
    for member, rows in out_blocks(core, x_here, out_mine, out_theirs):
        oa[member] = dot(rows, ctx_t[...], 1, 0)
    for member, y, half in blocks():
        lt[half * OP : (half + 1) * OP] = oa[member, y * OP : (y + 1) * OP]
    layer_out = patches[...].astype(F32) + lt[...].T
    token = lax.broadcasted_iota(jnp.int32, (CAP, 1), 0)
    outgoing = jnp.where(token < length, layer_out, 0.0).astype(BF)
    going = reorder(
        outgoing,
        lambda r: (r & 3) * OWNERS + ((NX * ((r >> 2) & 7) + (r >> 5) - offset) & (OWNERS - 1)),
    )
    for x in range(NX):
        rows_x[x] = going[x * EX : (x + 1) * EX]
    for step, out in enumerate(along):
        out[...] = rows_x[(x_here + step) & (NX - 1)]


def grads_kernel(got, normed, *refs):
    near, (send, fq, fo, tmp, rows_x) = refs[:NX], refs[NX:]
    x_here = lax.axis_index("x")
    total = None
    for member in range(TEAM):
        term = dot(got[member, 0:QB], normed[member], 1, 0)
        total = term if total is None else total + term
    fq[...] = total
    for lane in range(LB):
        low = QB + lane * OB
        total = got[0, low : low + OB].astype(F32)
        for member in range(1, TEAM):
            total += got[member, low : low + OB].astype(F32)
        fo[:, lane * CAP : (lane + 1) * CAP] = total
    for step, ref in enumerate(near):
        rows_x[(x_here - step) & (NX - 1)] = ref[...]
    rows = jnp.concatenate([rows_x[x] for x in range(NX)], axis=0)
    rows = reorder(rows, lambda r: ((r >> 2) & 3) * EX + (r >> 4) * W_EMB + (r & 3))
    for y in range(NY):
        tmp[0:QP] = fq[y * QP : (y + 1) * QP]
        tmp[QP:PIECE] = fo[y * OP : (y + 1) * OP]
        send[y, 0:EY] = rows[y * EY : (y + 1) * EY]
        send[y, EY : EY + PIECE] = tmp[...].astype(BF)


def terms_kernel(got, weights, mine, theirs):
    core = here()[0]
    for side, out in ((core, mine), (1 - core, theirs)):
        for x in range(NX):
            out[x] = dot(got[side * NX + x, 0:QB], weights[...], 0, 0).astype(BF)


def pair_kernel(mine, theirs, own, *others):
    x = lax.axis_index("x")
    for step, out in enumerate((own, *others)):
        image = (x + step) & (NX - 1)
        out[...] = (mine[image].astype(F32) + theirs[image].astype(F32)).astype(BF)


def patches_kernel(patches, grad, *refs):
    *terms, d_patches = refs
    d_normed = terms[0][...].astype(F32)
    for term in terms[1:]:
        d_normed += term[...].astype(F32)
    values_f, inverse, _ = normalize(patches[...])
    mean = jnp.mean(d_normed * values_f, axis=-1, keepdims=True)
    d_inputs = inverse * (d_normed - values_f * inverse * inverse * mean)
    d_patches[...] = (grad[...].astype(F32) + d_inputs).astype(BF)


def place_kernel(offsets, came, embeds):
    rows = jnp.concatenate([came[y, 0:EY] for y in range(NY)], axis=0)
    row = lax.broadcasted_iota(jnp.int32, (embeds.shape[0], CAP), 0)
    embeds[...] = dot(one_hot(row == target_rows(offsets)), rows, 1, 0).astype(BF)


def join_kernel(own, other, grad_qkv, grad_out):
    first = here()[0] == 0
    low = jnp.where(first, own[...], other[...])
    high = jnp.where(first, other[...], own[...])
    for out, rows in ((grad_qkv, slice(0, QP)), (grad_out, slice(QP, PIECE))):
        size = rows.stop - rows.start
        out[0:size] = low[rows]
        out[size : 2 * size] = high[rows]


def along_x(a, target):
    return lax.ppermute(a, "x", [(x, target(x)) for x in range(NX)])


def to_right(a, step):
    return along_x(a, lambda x: (x + step) % NX)


def swap(a):
    return lax.ppermute(a, "core", [(0, 1), (1, 0)])


def together(*arrays):
    return lax.optimization_barrier(arrays)


def exchange(a, axis):
    return lax.all_to_all(a, axis, split_axis=0, concat_axis=0, tiled=True)


def gather(a, axis):
    return lax.all_gather(a, axis, axis=0, tiled=True)


def local(patches, lengths, offsets, w_qkv, w_out, d_embeds):
    seq_rows = d_embeds.shape[0]
    tokens = patches.reshape(CAP, D)
    team = ("core", "x")
    scratch = pltpu.VMEM

    send = call(
        pre_kernel,
        sds((NY, EY + PIECE, D)),
        [
            scratch(d_embeds.shape, BF),
            scratch((2 * QP, D), BF),
            scratch((2 * OP, D), BF),
            pltpu.SemaphoreType.DMA((3,)),
            scratch((2 * QP, D), F32),
            scratch((2 * OP, D), F32),
        ],
        offsets, d_embeds, w_qkv.T, w_out.T, space=pltpu.HBM, limit=None,
    )
    got = exchange(send, "y")
    mine = gather(tokens, "x")
    theirs = swap(mine)
    send, w_block, out_block, normed = call(
        qkv_kernel,
        (sds((TEAM, QB + LB * EX, CAP)), sds((QB, D)), sds((OB, D)), sds((TEAM, CAP, D))),
        [scratch((PIECE, D), F32), scratch((QB, D), F32), scratch((OB, D), F32)],
        mine, theirs, got, smem=0,
    )
    got, *near = together(
        exchange(send, team), *[to_right(out_block, step) for step in range(1, NX)]
    )
    out_mine = jnp.concatenate([out_block, *near], axis=0)
    out_theirs = swap(out_mine)
    qkv_t, prob, ctx_t, context = call(
        fwd_kernel,
        (sds((3 * D, CAP)), sds((HEADS, CAP, CAP), F32), sds((D, CAP)), sds((CAP, D))),
        [scratch((3 * D, CAP), F32), scratch((3 * D, CAP), F32)],
        lengths, got,
    )
    send, grad = call(
        bwd_kernel,
        (sds((TEAM, QB + LB * OB, CAP)), sds((CAP, D))),
        [
            scratch((D, CAP), F32),
            scratch((TEAM, OB, CAP), F32),
            scratch((3 * D, CAP), F32),
            scratch((3 * D, CAP), F32),
        ],
        lengths, offsets, got, qkv_t, prob, context, out_mine, out_theirs, smem=2,
    )
    send, ctx_t = together(send, ctx_t)
    rows_x = scratch((NX, EX, D), BF)
    along = call(
        out_kernel,
        (sds((EX, D)),) * NX,
        [scratch((D, CAP), F32), scratch((TEAM, OB, CAP), F32), rows_x],
        lengths, offsets, tokens, ctx_t, out_mine, out_theirs, smem=2,
    )
    near = [a if step == 0 else to_right(a, step) for step, a in enumerate(along)]
    got, *near = together(exchange(send, team), *near)
    send = call(
        grads_kernel,
        sds((NY, EY + PIECE, D)),
        [scratch((QB, D), F32), scratch((OB, D), F32), scratch((PIECE, D), F32), rows_x],
        got, normed, *near, smem=0,
    )
    send, got = together(send, got)
    term, other = call(
        terms_kernel,
        (sds((NX, CAP, D)), sds((NX, CAP, D))),
        [], got, w_block, smem=0,
    )
    got = exchange(send, "y")
    own, right, across, left = call(
        pair_kernel, (sds((CAP, D)),) * NX, [], term, swap(other), smem=0
    )
    got, right, across, left = together(got, to_right(right, 1), across, left)
    terms = own, right, to_right(across, 2), to_right(left, NX - 1)
    embeds = call(place_kernel, sds((seq_rows, D)), [], offsets, got)
    total = jnp.sum(got[:, EY:].astype(F32), axis=0).astype(BF)
    got = exchange(jnp.broadcast_to(total[None], (NZ, PIECE, D)), "z")
    d_patches = call(
        patches_kernel, sds((CAP, D)), [],
        tokens, grad, *terms, smem=0,
    )
    got, d_patches, embeds = together(got, d_patches, embeds)
    factor = 1.0 / math.sqrt(CAP * OWNERS * 2 * NZ)
    own = jnp.sum(got.astype(F32), axis=0) * factor
    other = swap(own)
    grad_qkv, grad_out = call(
        join_kernel, (sds((2 * QP, D), F32), sds((2 * OP, D), F32)), [], own, other, smem=0
    )
    return embeds, d_patches.reshape(patches.shape), grad_qkv.T, grad_out.T


def solution(mesh):
    axes = Mesh(mesh.devices.reshape(NZ, 2, NY, NX), ("z", "core", "y", "x"))
    group, plane = ("z", "core"), ("y", "x")
    return jax.shard_map(
        local,
        mesh=axes,
        in_specs=(
            P(group + plane, None, None),
            P(group),
            P(group),
            P(None, plane),
            P(None, plane),
            P(group + plane, None),
        ),
        out_specs=(
            P(group + plane, None),
            P(group + plane, None, None),
            P(None, plane),
            P(None, plane),
        ),
        check_vma=False,
    )
```

```python
import math

import jax
import jax.numpy as jnp
from jax import lax
from jax.experimental import pallas as pl
from jax.experimental.pallas import tpu as pltpu
from jax.sharding import Mesh, PartitionSpec as P

HEADS = 8
HEAD_DIM = 80
D = 640
CAP = 128
NX, NY, NZ = 4, 8, 8
OWNERS = NX * NY
QP, OP = 30, 10
PIECE = QP + OP
W_EMB = CAP // OWNERS
EX = NY * W_EMB
EY = NX * W_EMB
SCALE = HEAD_DIM ** (-0.5)
BF = jnp.bfloat16
F32 = jnp.float32
VMEM_LIMIT = 20 * 1024 * 1024
TEAM = 2 * NX
QB, OB = NY * QP, NY * OP
LB = D // CAP


def dot(a, b, ca, cb):
    return lax.dot_general(a, b, (((ca,), (cb,)), ((), ())), preferred_element_type=F32)


def call(kernel, out_shape, scratch, *args, smem=1, limit=VMEM_LIMIT):
    specs = [pl.BlockSpec(memory_space=pltpu.SMEM)] * smem + [
        pl.BlockSpec(memory_space=pltpu.VMEM)
    ] * (len(args) - smem)
    return pl.pallas_call(
        kernel,
        out_shape=out_shape,
        in_specs=specs,
        out_specs=jax.tree.map(lambda _: pl.BlockSpec(memory_space=pltpu.VMEM), out_shape),
        scratch_shapes=scratch,
        compiler_params=pltpu.CompilerParams(vmem_limit_bytes=limit),
    )(*args)


def sds(shape, dtype=BF):
    return jax.ShapeDtypeStruct(shape, dtype)


def here():
    return lax.axis_index("core"), lax.axis_index("y") * NX + lax.axis_index("x")


def target_rows(offsets):
    owner = here()[1]
    lane = lax.broadcasted_iota(jnp.int32, (1, CAP), 1)
    offset = jnp.zeros((1, CAP), jnp.int32)
    for image in range(OWNERS):
        offset = jnp.where(lane >> 2 == image, offsets[image], offset)
    return ((offset + ((owner - offset) & (OWNERS - 1))) >> 5) + (lane & (W_EMB - 1))


def one_hot(hit):
    return hit.astype(F32).astype(BF)


def reorder(rows, source):
    row = lax.broadcasted_iota(jnp.int32, (CAP, CAP), 0)
    column = lax.broadcasted_iota(jnp.int32, (CAP, CAP), 1)
    return dot(one_hot(column == source(row)), rows, 1, 0).astype(BF)


def put_rows(ref, first, rows):
    core = here()[0]
    for x in range(NX):
        for lane in range(LB):
            part = rows[x * EX : (x + 1) * EX, lane * CAP : (lane + 1) * CAP]
            ref[core * NX + x, first + lane * EX : first + (lane + 1) * EX] = part
        ref[(1 - core) * NX + x, first : first + LB * EX] = jnp.zeros((LB * EX, CAP), BF)


def get_rows(ref, first):
    core = here()[0]
    parts = []
    for x in range(NX):
        lanes = [
            ref[core * NX + x, first + lane * EX : first + (lane + 1) * EX] for lane in range(LB)
        ]
        parts.append(jnp.concatenate(lanes, axis=1))
    return jnp.concatenate(parts, axis=0)


def blocks():
    for core in range(2):
        for x in range(NX):
            for y in range(NY):
                yield core * NX + x, y, 2 * (NX * y + x) + core


def pre_kernel(offsets, d_embeds, wq, wo, send, fq, fo):
    first = here()[0] == 0
    row = lax.broadcasted_iota(jnp.int32, (d_embeds.shape[0], CAP), 0)
    pick = one_hot(row == target_rows(offsets))
    fetched = dot(pick, d_embeds[...], 0, 0).astype(BF)
    fq[...] = wq[...].astype(F32)
    fo[...] = wo[...].astype(F32)
    half_q = jnp.where(first, fq[0:QP], fq[QP : 2 * QP])
    half_o = jnp.where(first, fo[0:OP], fo[OP : 2 * OP])
    fq[0:QP] = half_q
    fq[QP:PIECE] = half_o
    piece = fq[0:PIECE].astype(BF)
    for y in range(NY):
        send[y, 0:EY] = fetched[y * EY : (y + 1) * EY]
        send[y, EY : EY + PIECE] = piece


def normalize(patches):
    values_f = patches.astype(F32)
    inverse = lax.rsqrt(jnp.mean(values_f * values_f, axis=-1, keepdims=True) + 1e-06)
    return values_f, inverse, (values_f * inverse).astype(BF)


def qkv_kernel(mine, theirs, got, send, w_block, out_block, normed, tmp, fq, fo):
    core = here()[0]
    for y in range(NY):
        tmp[...] = got[y, EY : EY + PIECE].astype(F32)
        fq[y * QP : (y + 1) * QP] = tmp[0:QP]
        fo[y * OP : (y + 1) * OP] = tmp[QP:PIECE]
    weights = fq[...].astype(BF)
    w_block[...] = weights
    out_block[...] = fo[...].astype(BF)
    for side, patches in ((core, mine), (1 - core, theirs)):
        for x in range(NX):
            member = side * NX + x
            low = normalize(patches[x * CAP : (x + 1) * CAP])[2]
            normed[member] = low
            send[member, 0:QB] = dot(weights, low, 1, 1).astype(BF)
    rows = jnp.concatenate([got[y, 0:EY] for y in range(NY)], axis=0)
    rows = reorder(rows, lambda r: ((r >> 2) & 7) * EY + (r >> 5) * W_EMB + (r & 3))
    put_rows(send, QB, rows)


def fwd_kernel(lengths, got, qkv_t, prob, ctx_t, context, pa, qf):
    length = lengths[here()[1]]
    for member in range(TEAM):
        pa[member * QB : (member + 1) * QB] = got[member, 0:QB].astype(F32)
    for member, y, half in blocks():
        low = member * QB + y * QP
        qf[half * QP : (half + 1) * QP] = pa[low : low + QP]
    qkv_t[...] = qf[...].astype(BF)
    allowed = lax.broadcasted_iota(jnp.int32, (CAP, CAP), 1) < length
    for h in range(HEADS):
        q, k, v = (
            qkv_t[part * D + h * HEAD_DIM : part * D + (h + 1) * HEAD_DIM] for part in range(3)
        )
        scores = jnp.where(allowed, dot(q, k, 0, 0) * SCALE, -1e30)
        highest = jnp.max(scores, axis=-1, keepdims=True)
        weights = jnp.where(allowed, jnp.exp(scores - highest), 0.0)
        weights = weights / jnp.sum(weights, axis=-1, keepdims=True)
        prob[h] = weights
        ctx_t[h * HEAD_DIM : (h + 1) * HEAD_DIM] = dot(v, weights.astype(BF), 1, 1).astype(BF)
    context[...] = ctx_t[...].astype(F32).T.astype(BF)


def out_blocks(core, x_here, mine, theirs):
    for side, ref in ((core, mine), (1 - core, theirs)):
        for step in range(NX):
            member = side * NX + ((x_here - step) & (NX - 1))
            yield member, ref[step * OB : (step + 1) * OB]


def bwd_kernel(
    lengths, offsets, got, qkv_t, prob, context, out_mine, out_theirs, send,
    grad, gt, gp, dq, dp,
):
    core, me = here()
    x_here = lax.axis_index("x")
    length, offset = lengths[me], offsets[me]
    came = get_rows(got, QB)
    slot = lax.broadcasted_iota(jnp.int32, (CAP, CAP), 0)
    owner = (slot + offset) & (OWNERS - 1)
    source = (owner & 3) * EX + (owner >> 2) * W_EMB + (slot >> 5)
    column = lax.broadcasted_iota(jnp.int32, (CAP, CAP), 1)
    grad_f = dot(one_hot((column == source) & (slot < length)), came, 1, 0)
    grad[...] = grad_f.astype(BF)
    gt[...] = grad_f.T
    for member, y, half in blocks():
        gp[member, y * OP : (y + 1) * OP] = gt[half * OP : (half + 1) * OP]
    d_ctx = None
    for member, rows in out_blocks(core, x_here, out_mine, out_theirs):
        term = dot(gp[member].T.astype(BF), rows, 1, 0)
        d_ctx = term if d_ctx is None else d_ctx + term
    d_ctx_t = d_ctx.astype(BF).astype(F32).T.astype(BF)
    for h in range(HEADS):
        at = [slice(part * D + h * HEAD_DIM, part * D + (h + 1) * HEAD_DIM) for part in range(3)]
        q, k, v = (qkv_t[rows] for rows in at)
        dc = d_ctx_t[h * HEAD_DIM : (h + 1) * HEAD_DIM]
        weights = prob[h]
        d_prob = dot(dc, v, 0, 0)
        dq[at[2]] = dot(dc, weights.astype(BF), 1, 0)
        inner = jnp.sum(d_prob * weights, axis=-1, keepdims=True)
        d_scores = (weights * (d_prob - inner) * SCALE).astype(BF)
        dq[at[0]] = dot(k, d_scores, 1, 1)
        dq[at[1]] = dot(q, d_scores, 1, 0)
    for member, y, half in blocks():
        low = member * QB + y * QP
        dp[low : low + QP] = dq[half * QP : (half + 1) * QP]
    for member in range(TEAM):
        send[member, 0:QB] = dp[member * QB : (member + 1) * QB].astype(BF)
        rows = gp[member].astype(BF)
        part = dot(rows, context[...], 1, 0).astype(BF)
        for lane in range(LB):
            low = QB + lane * OB
            send[member, low : low + OB] = part[:, lane * CAP : (lane + 1) * CAP]


def out_kernel(lengths, offsets, patches, ctx_t, out_mine, out_theirs, *refs):
    along, (lt, oa, rows_x) = refs[:NX], refs[NX:]
    core, me = here()
    x_here = lax.axis_index("x")
    length, offset = lengths[me], offsets[me]
    for member, rows in out_blocks(core, x_here, out_mine, out_theirs):
        oa[member] = dot(rows, ctx_t[...], 1, 0)
    for member, y, half in blocks():
        lt[half * OP : (half + 1) * OP] = oa[member, y * OP : (y + 1) * OP]
    layer_out = patches[...].astype(F32) + lt[...].T
    token = lax.broadcasted_iota(jnp.int32, (CAP, 1), 0)
    outgoing = jnp.where(token < length, layer_out, 0.0).astype(BF)
    going = reorder(
        outgoing,
        lambda r: (r & 3) * OWNERS + ((NX * ((r >> 2) & 7) + (r >> 5) - offset) & (OWNERS - 1)),
    )
    for x in range(NX):
        rows_x[x] = going[x * EX : (x + 1) * EX]
    for step, out in enumerate(along):
        out[...] = rows_x[(x_here + step) & (NX - 1)]


def grads_kernel(got, normed, *refs):
    near, (send, fq, fo, tmp, rows_x) = refs[:NX], refs[NX:]
    x_here = lax.axis_index("x")
    total = None
    for member in range(TEAM):
        term = dot(got[member, 0:QB], normed[member], 1, 0)
        total = term if total is None else total + term
    fq[...] = total
    for lane in range(LB):
        low = QB + lane * OB
        total = got[0, low : low + OB].astype(F32)
        for member in range(1, TEAM):
            total += got[member, low : low + OB].astype(F32)
        fo[:, lane * CAP : (lane + 1) * CAP] = total
    for step, ref in enumerate(near):
        rows_x[(x_here - step) & (NX - 1)] = ref[...]
    rows = jnp.concatenate([rows_x[x] for x in range(NX)], axis=0)
    rows = reorder(rows, lambda r: ((r >> 2) & 3) * EX + (r >> 4) * W_EMB + (r & 3))
    for y in range(NY):
        tmp[0:QP] = fq[y * QP : (y + 1) * QP]
        tmp[QP:PIECE] = fo[y * OP : (y + 1) * OP]
        send[y, 0:EY] = rows[y * EY : (y + 1) * EY]
        send[y, EY : EY + PIECE] = tmp[...].astype(BF)


def terms_kernel(got, weights, mine, theirs):
    core = here()[0]
    for side, out in ((core, mine), (1 - core, theirs)):
        for x in range(NX):
            out[x] = dot(got[side * NX + x, 0:QB], weights[...], 0, 0).astype(BF)


def pair_kernel(mine, theirs, own, *others):
    x = lax.axis_index("x")
    for step, out in enumerate((own, *others)):
        image = (x + step) & (NX - 1)
        out[...] = (mine[image].astype(F32) + theirs[image].astype(F32)).astype(BF)


def patches_kernel(patches, grad, *refs):
    *terms, d_patches = refs
    d_normed = terms[0][...].astype(F32)
    for term in terms[1:]:
        d_normed += term[...].astype(F32)
    values_f, inverse, _ = normalize(patches[...])
    mean = jnp.mean(d_normed * values_f, axis=-1, keepdims=True)
    d_inputs = inverse * (d_normed - values_f * inverse * inverse * mean)
    d_patches[...] = (grad[...].astype(F32) + d_inputs).astype(BF)


def place_kernel(offsets, came, embeds):
    rows = jnp.concatenate([came[y, 0:EY] for y in range(NY)], axis=0)
    row = lax.broadcasted_iota(jnp.int32, (embeds.shape[0], CAP), 0)
    embeds[...] = dot(one_hot(row == target_rows(offsets)), rows, 1, 0).astype(BF)


def join_kernel(own, other, grad_qkv, grad_out):
    first = here()[0] == 0
    low = jnp.where(first, own[...], other[...])
    high = jnp.where(first, other[...], own[...])
    for out, rows in ((grad_qkv, slice(0, QP)), (grad_out, slice(QP, PIECE))):
        size = rows.stop - rows.start
        out[0:size] = low[rows]
        out[size : 2 * size] = high[rows]


def along_x(a, target):
    return lax.ppermute(a, "x", [(x, target(x)) for x in range(NX)])


def to_right(a, step):
    return along_x(a, lambda x: (x + step) % NX)


def swap(a):
    return lax.ppermute(a, "core", [(0, 1), (1, 0)])


def together(*arrays):
    return lax.optimization_barrier(arrays)


def exchange(a, axis):
    return lax.all_to_all(a, axis, split_axis=0, concat_axis=0, tiled=True)


def gather(a, axis):
    return lax.all_gather(a, axis, axis=0, tiled=True)


def local(patches, lengths, offsets, w_qkv, w_out, d_embeds):
    seq_rows = d_embeds.shape[0]
    tokens = patches.reshape(CAP, D)
    team = ("core", "x")
    scratch = pltpu.VMEM

    send = call(
        pre_kernel,
        sds((NY, EY + PIECE, D)),
        [scratch((2 * QP, D), F32), scratch((2 * OP, D), F32)],
        offsets, d_embeds, w_qkv.T, w_out.T, limit=56 * 1024 * 1024,
    )
    got = exchange(send, "y")
    mine = gather(tokens, "x")
    theirs = swap(mine)
    send, w_block, out_block, normed = call(
        qkv_kernel,
        (sds((TEAM, QB + LB * EX, CAP)), sds((QB, D)), sds((OB, D)), sds((TEAM, CAP, D))),
        [scratch((PIECE, D), F32), scratch((QB, D), F32), scratch((OB, D), F32)],
        mine, theirs, got, smem=0,
    )
    got, *near = together(
        exchange(send, team), *[to_right(out_block, step) for step in range(1, NX)]
    )
    out_mine = jnp.concatenate([out_block, *near], axis=0)
    out_theirs = swap(out_mine)
    qkv_t, prob, ctx_t, context = call(
        fwd_kernel,
        (sds((3 * D, CAP)), sds((HEADS, CAP, CAP), F32), sds((D, CAP)), sds((CAP, D))),
        [scratch((3 * D, CAP), F32), scratch((3 * D, CAP), F32)],
        lengths, got,
    )
    send, grad = call(
        bwd_kernel,
        (sds((TEAM, QB + LB * OB, CAP)), sds((CAP, D))),
        [
            scratch((D, CAP), F32),
            scratch((TEAM, OB, CAP), F32),
            scratch((3 * D, CAP), F32),
            scratch((3 * D, CAP), F32),
        ],
        lengths, offsets, got, qkv_t, prob, context, out_mine, out_theirs, smem=2,
    )
    send, ctx_t = together(send, ctx_t)
    rows_x = scratch((NX, EX, D), BF)
    along = call(
        out_kernel,
        (sds((EX, D)),) * NX,
        [scratch((D, CAP), F32), scratch((TEAM, OB, CAP), F32), rows_x],
        lengths, offsets, tokens, ctx_t, out_mine, out_theirs, smem=2,
    )
    near = [a if step == 0 else to_right(a, step) for step, a in enumerate(along)]
    got, *near = together(exchange(send, team), *near)
    send = call(
        grads_kernel,
        sds((NY, EY + PIECE, D)),
        [scratch((QB, D), F32), scratch((OB, D), F32), scratch((PIECE, D), F32), rows_x],
        got, normed, *near, smem=0,
    )
    send, got = together(send, got)
    term, other = call(
        terms_kernel,
        (sds((NX, CAP, D)), sds((NX, CAP, D))),
        [], got, w_block, smem=0,
    )
    got = exchange(send, "y")
    own, right, across, left = call(
        pair_kernel, (sds((CAP, D)),) * NX, [], term, swap(other), smem=0
    )
    got, right, across, left = together(got, to_right(right, 1), across, left)
    terms = own, right, to_right(across, 2), to_right(left, NX - 1)
    embeds = call(place_kernel, sds((seq_rows, D)), [], offsets, got)
    total = jnp.sum(got[:, EY:].astype(F32), axis=0).astype(BF)
    got = exchange(jnp.broadcast_to(total[None], (NZ, PIECE, D)), "z")
    d_patches = call(
        patches_kernel, sds((CAP, D)), [],
        tokens, grad, *terms, smem=0,
    )
    got, d_patches, embeds = together(got, d_patches, embeds)
    factor = 1.0 / math.sqrt(CAP * OWNERS * 2 * NZ)
    own = jnp.sum(got.astype(F32), axis=0) * factor
    other = swap(own)
    grad_qkv, grad_out = call(
        join_kernel, (sds((2 * QP, D), F32), sds((2 * OP, D), F32)), [], own, other, smem=0
    )
    return embeds, d_patches.reshape(patches.shape), grad_qkv.T, grad_out.T


def solution(mesh):
    axes = Mesh(mesh.devices.reshape(NZ, 2, NY, NX), ("z", "core", "y", "x"))
    group, plane = ("z", "core"), ("y", "x")
    return jax.shard_map(
        local,
        mesh=axes,
        in_specs=(
            P(group + plane, None, None),
            P(group),
            P(group),
            P(None, plane),
            P(None, plane),
            P(group + plane, None),
        ),
        out_specs=(
            P(group + plane, None),
            P(group + plane, None, None),
            P(None, plane),
            P(None, plane),
        ),
        check_vma=False,
    )
```

```python
import math

import jax
import jax.numpy as jnp
from jax import lax
from jax.experimental import pallas as pl
from jax.experimental.pallas import tpu as pltpu
from jax.sharding import Mesh, PartitionSpec as P

HEADS = 8
HEAD_DIM = 80
D = 640
CAP = 128
NX, NY, NZ = 4, 8, 8
OWNERS = NX * NY
QP, OP = 30, 10
PIECE = QP + OP
W_EMB = CAP // OWNERS
EX = NY * W_EMB
EY = NX * W_EMB
SCALE = HEAD_DIM ** (-0.5)
BF = jnp.bfloat16
F32 = jnp.float32
VMEM_LIMIT = 20 * 1024 * 1024
TEAM = 2 * NX
QB, OB = NY * QP, NY * OP
LB = D // CAP


def dot(a, b, ca, cb):
    return lax.dot_general(a, b, (((ca,), (cb,)), ((), ())), preferred_element_type=F32)


def call(kernel, out_shape, scratch, *args, smem=1, limit=VMEM_LIMIT):
    specs = [pl.BlockSpec(memory_space=pltpu.SMEM)] * smem + [
        pl.BlockSpec(memory_space=pltpu.VMEM)
    ] * (len(args) - smem)
    return pl.pallas_call(
        kernel,
        out_shape=out_shape,
        in_specs=specs,
        out_specs=jax.tree.map(lambda _: pl.BlockSpec(memory_space=pltpu.VMEM), out_shape),
        scratch_shapes=scratch,
        compiler_params=pltpu.CompilerParams(vmem_limit_bytes=limit),
    )(*args)


def sds(shape, dtype=BF):
    return jax.ShapeDtypeStruct(shape, dtype)


def here():
    return lax.axis_index("core"), lax.axis_index("y") * NX + lax.axis_index("x")


def target_rows(offsets):
    owner = here()[1]
    lane = lax.broadcasted_iota(jnp.int32, (1, CAP), 1)
    offset = jnp.zeros((1, CAP), jnp.int32)
    for image in range(OWNERS):
        offset = jnp.where(lane >> 2 == image, offsets[image], offset)
    return ((offset + ((owner - offset) & (OWNERS - 1))) >> 5) + (lane & (W_EMB - 1))


def one_hot(hit):
    return hit.astype(F32).astype(BF)


def reorder(rows, source):
    row = lax.broadcasted_iota(jnp.int32, (CAP, CAP), 0)
    column = lax.broadcasted_iota(jnp.int32, (CAP, CAP), 1)
    return dot(one_hot(column == source(row)), rows, 1, 0).astype(BF)


def put_rows(ref, first, rows):
    core = here()[0]
    for x in range(NX):
        for lane in range(LB):
            part = rows[x * EX : (x + 1) * EX, lane * CAP : (lane + 1) * CAP]
            ref[core * NX + x, first + lane * EX : first + (lane + 1) * EX] = part
        ref[(1 - core) * NX + x, first : first + LB * EX] = jnp.zeros((LB * EX, CAP), BF)


def get_rows(ref, first):
    core = here()[0]
    parts = []
    for x in range(NX):
        lanes = [
            ref[core * NX + x, first + lane * EX : first + (lane + 1) * EX] for lane in range(LB)
        ]
        parts.append(jnp.concatenate(lanes, axis=1))
    return jnp.concatenate(parts, axis=0)


def blocks():
    for core in range(2):
        for x in range(NX):
            for y in range(NY):
                yield core * NX + x, y, 2 * (NX * y + x) + core


def pre_kernel(offsets, d_embeds, wq, wo, send, fq, fo):
    first = here()[0] == 0
    row = lax.broadcasted_iota(jnp.int32, (d_embeds.shape[0], CAP), 0)
    pick = one_hot(row == target_rows(offsets))
    fetched = dot(pick, d_embeds[...], 0, 0).astype(BF)
    fq[...] = wq[...].astype(F32)
    fo[...] = wo[...].astype(F32)
    half_q = jnp.where(first, fq[0:QP], fq[QP : 2 * QP])
    half_o = jnp.where(first, fo[0:OP], fo[OP : 2 * OP])
    fq[0:QP] = half_q
    fq[QP:PIECE] = half_o
    piece = fq[0:PIECE].astype(BF)
    for y in range(NY):
        send[y, 0:EY] = fetched[y * EY : (y + 1) * EY]
        send[y, EY : EY + PIECE] = piece


def normalize(patches):
    values_f = patches.astype(F32)
    inverse = lax.rsqrt(jnp.mean(values_f * values_f, axis=-1, keepdims=True) + 1e-06)
    return values_f, inverse, (values_f * inverse).astype(BF)


def qkv_kernel(mine, theirs, got, send, w_block, out_block, normed, tmp, fq, fo):
    core = here()[0]
    for y in range(NY):
        tmp[...] = got[y, EY : EY + PIECE].astype(F32)
        fq[y * QP : (y + 1) * QP] = tmp[0:QP]
        fo[y * OP : (y + 1) * OP] = tmp[QP:PIECE]
    weights = fq[...].astype(BF)
    w_block[...] = weights
    out_block[...] = fo[...].astype(BF)
    for side, patches in ((core, mine), (1 - core, theirs)):
        for x in range(NX):
            member = side * NX + x
            low = normalize(patches[x * CAP : (x + 1) * CAP])[2]
            normed[member] = low
            send[member, 0:QB] = dot(weights, low, 1, 1).astype(BF)
    rows = jnp.concatenate([got[y, 0:EY] for y in range(NY)], axis=0)
    rows = reorder(rows, lambda r: ((r >> 2) & 7) * EY + (r >> 5) * W_EMB + (r & 3))
    put_rows(send, QB, rows)


def fwd_kernel(lengths, got, qkv_t, prob, ctx_t, context, pa, qf):
    length = lengths[here()[1]]
    for member in range(TEAM):
        pa[member * QB : (member + 1) * QB] = got[member, 0:QB].astype(F32)
    for member, y, half in blocks():
        low = member * QB + y * QP
        qf[half * QP : (half + 1) * QP] = pa[low : low + QP]
    qkv_t[...] = qf[...].astype(BF)
    allowed = lax.broadcasted_iota(jnp.int32, (CAP, CAP), 1) < length
    for h in range(HEADS):
        q, k, v = (
            qkv_t[part * D + h * HEAD_DIM : part * D + (h + 1) * HEAD_DIM] for part in range(3)
        )
        scores = jnp.where(allowed, dot(q, k, 0, 0) * SCALE, -1e30)
        highest = jnp.max(scores, axis=-1, keepdims=True)
        weights = jnp.where(allowed, jnp.exp(scores - highest), 0.0)
        weights = weights / jnp.sum(weights, axis=-1, keepdims=True)
        prob[h] = weights
        ctx_t[h * HEAD_DIM : (h + 1) * HEAD_DIM] = dot(v, weights.astype(BF), 1, 1).astype(BF)
    context[...] = ctx_t[...].astype(F32).T.astype(BF)


def out_blocks(core, x_here, mine, theirs):
    for side, ref in ((core, mine), (1 - core, theirs)):
        for step in range(NX):
            member = side * NX + ((x_here - step) & (NX - 1))
            yield member, ref[step * OB : (step + 1) * OB]


def bwd_kernel(
    lengths, offsets, got, qkv_t, prob, context, out_mine, out_theirs, send,
    grad, gt, gp, go, dq, dp,
):
    core, me = here()
    x_here = lax.axis_index("x")
    length, offset = lengths[me], offsets[me]
    came = get_rows(got, QB)
    slot = lax.broadcasted_iota(jnp.int32, (CAP, CAP), 0)
    owner = (slot + offset) & (OWNERS - 1)
    source = (owner & 3) * EX + (owner >> 2) * W_EMB + (slot >> 5)
    column = lax.broadcasted_iota(jnp.int32, (CAP, CAP), 1)
    grad_f = dot(one_hot((column == source) & (slot < length)), came, 1, 0)
    grad[...] = grad_f.astype(BF)
    gt[...] = grad_f.T
    for member, y, half in blocks():
        gp[member, y * OP : (y + 1) * OP] = gt[half * OP : (half + 1) * OP]
    for n, (member, _) in enumerate(out_blocks(core, x_here, out_mine, out_theirs)):
        go[n] = gp[member]
    left = go[...].reshape(TEAM * OB, CAP).T.astype(BF)
    rows = jnp.concatenate([out_mine[...], out_theirs[...]], axis=0)
    d_ctx = dot(left, rows, 1, 0)
    d_ctx_t = d_ctx.astype(BF).astype(F32).T.astype(BF)
    for h in range(HEADS):
        at = [slice(part * D + h * HEAD_DIM, part * D + (h + 1) * HEAD_DIM) for part in range(3)]
        q, k, v = (qkv_t[rows] for rows in at)
        dc = d_ctx_t[h * HEAD_DIM : (h + 1) * HEAD_DIM]
        weights = prob[h]
        d_prob = dot(dc, v, 0, 0)
        dq[at[2]] = dot(dc, weights.astype(BF), 1, 0)
        inner = jnp.sum(d_prob * weights, axis=-1, keepdims=True)
        d_scores = (weights * (d_prob - inner) * SCALE).astype(BF)
        dq[at[0]] = dot(k, d_scores, 1, 1)
        dq[at[1]] = dot(q, d_scores, 1, 0)
    for member, y, half in blocks():
        low = member * QB + y * QP
        dp[low : low + QP] = dq[half * QP : (half + 1) * QP]
    parts = dot(gp[...].reshape(TEAM * OB, CAP).astype(BF), context[...], 1, 0).astype(BF)
    for member in range(TEAM):
        send[member, 0:QB] = dp[member * QB : (member + 1) * QB].astype(BF)
        part = parts[member * OB : (member + 1) * OB]
        for lane in range(LB):
            low = QB + lane * OB
            send[member, low : low + OB] = part[:, lane * CAP : (lane + 1) * CAP]


def out_kernel(lengths, offsets, patches, ctx_t, out_mine, out_theirs, *refs):
    along, (lt, oa, rows_x) = refs[:NX], refs[NX:]
    core, me = here()
    x_here = lax.axis_index("x")
    length, offset = lengths[me], offsets[me]
    for member, rows in out_blocks(core, x_here, out_mine, out_theirs):
        oa[member] = dot(rows, ctx_t[...], 1, 0)
    for member, y, half in blocks():
        lt[half * OP : (half + 1) * OP] = oa[member, y * OP : (y + 1) * OP]
    layer_out = patches[...].astype(F32) + lt[...].T
    token = lax.broadcasted_iota(jnp.int32, (CAP, 1), 0)
    outgoing = jnp.where(token < length, layer_out, 0.0).astype(BF)
    going = reorder(
        outgoing,
        lambda r: (r & 3) * OWNERS + ((NX * ((r >> 2) & 7) + (r >> 5) - offset) & (OWNERS - 1)),
    )
    for x in range(NX):
        rows_x[x] = going[x * EX : (x + 1) * EX]
    for step, out in enumerate(along):
        out[...] = rows_x[(x_here + step) & (NX - 1)]


def grads_kernel(got, normed, *refs):
    near, (send, fq, fo, tmp, rows_x) = refs[:NX], refs[NX:]
    x_here = lax.axis_index("x")
    left = jnp.concatenate([got[member, 0:QB] for member in range(TEAM)], axis=1)
    fq[...] = dot(left, normed[...].reshape(TEAM * CAP, D), 1, 0)
    for lane in range(LB):
        low = QB + lane * OB
        total = got[0, low : low + OB].astype(F32)
        for member in range(1, TEAM):
            total += got[member, low : low + OB].astype(F32)
        fo[:, lane * CAP : (lane + 1) * CAP] = total
    for step, ref in enumerate(near):
        rows_x[(x_here - step) & (NX - 1)] = ref[...]
    rows = jnp.concatenate([rows_x[x] for x in range(NX)], axis=0)
    rows = reorder(rows, lambda r: ((r >> 2) & 3) * EX + (r >> 4) * W_EMB + (r & 3))
    for y in range(NY):
        tmp[0:QP] = fq[y * QP : (y + 1) * QP]
        tmp[QP:PIECE] = fo[y * OP : (y + 1) * OP]
        send[y, 0:EY] = rows[y * EY : (y + 1) * EY]
        send[y, EY : EY + PIECE] = tmp[...].astype(BF)


def terms_kernel(got, weights, mine, theirs):
    core = here()[0]
    for side, out in ((core, mine), (1 - core, theirs)):
        for x in range(NX):
            out[x] = dot(got[side * NX + x, 0:QB], weights[...], 0, 0).astype(BF)


def pair_kernel(mine, theirs, own, *others):
    x = lax.axis_index("x")
    for step, out in enumerate((own, *others)):
        image = (x + step) & (NX - 1)
        out[...] = (mine[image].astype(F32) + theirs[image].astype(F32)).astype(BF)


def patches_kernel(patches, grad, *refs):
    *terms, d_patches = refs
    d_normed = terms[0][...].astype(F32)
    for term in terms[1:]:
        d_normed += term[...].astype(F32)
    values_f, inverse, _ = normalize(patches[...])
    mean = jnp.mean(d_normed * values_f, axis=-1, keepdims=True)
    d_inputs = inverse * (d_normed - values_f * inverse * inverse * mean)
    d_patches[...] = (grad[...].astype(F32) + d_inputs).astype(BF)


def place_kernel(offsets, came, embeds):
    rows = jnp.concatenate([came[y, 0:EY] for y in range(NY)], axis=0)
    row = lax.broadcasted_iota(jnp.int32, (embeds.shape[0], CAP), 0)
    embeds[...] = dot(one_hot(row == target_rows(offsets)), rows, 1, 0).astype(BF)


def join_kernel(own, other, grad_qkv, grad_out):
    first = here()[0] == 0
    low = jnp.where(first, own[...], other[...])
    high = jnp.where(first, other[...], own[...])
    for out, rows in ((grad_qkv, slice(0, QP)), (grad_out, slice(QP, PIECE))):
        size = rows.stop - rows.start
        out[0:size] = low[rows]
        out[size : 2 * size] = high[rows]


def along_x(a, target):
    return lax.ppermute(a, "x", [(x, target(x)) for x in range(NX)])


def to_right(a, step):
    return along_x(a, lambda x: (x + step) % NX)


def swap(a):
    return lax.ppermute(a, "core", [(0, 1), (1, 0)])


def together(*arrays):
    return lax.optimization_barrier(arrays)


def exchange(a, axis):
    return lax.all_to_all(a, axis, split_axis=0, concat_axis=0, tiled=True)


def gather(a, axis):
    return lax.all_gather(a, axis, axis=0, tiled=True)


def local(patches, lengths, offsets, w_qkv, w_out, d_embeds):
    seq_rows = d_embeds.shape[0]
    tokens = patches.reshape(CAP, D)
    team = ("core", "x")
    scratch = pltpu.VMEM

    send = call(
        pre_kernel,
        sds((NY, EY + PIECE, D)),
        [scratch((2 * QP, D), F32), scratch((2 * OP, D), F32)],
        offsets, d_embeds, w_qkv.T, w_out.T, limit=56 * 1024 * 1024,
    )
    got = exchange(send, "y")
    mine = gather(tokens, "x")
    theirs = swap(mine)
    send, w_block, out_block, normed = call(
        qkv_kernel,
        (sds((TEAM, QB + LB * EX, CAP)), sds((QB, D)), sds((OB, D)), sds((TEAM, CAP, D))),
        [scratch((PIECE, D), F32), scratch((QB, D), F32), scratch((OB, D), F32)],
        mine, theirs, got, smem=0,
    )
    got, *near = together(
        exchange(send, team), *[to_right(out_block, step) for step in range(1, NX)]
    )
    out_mine = jnp.concatenate([out_block, *near], axis=0)
    out_theirs = swap(out_mine)
    qkv_t, prob, ctx_t, context = call(
        fwd_kernel,
        (sds((3 * D, CAP)), sds((HEADS, CAP, CAP), F32), sds((D, CAP)), sds((CAP, D))),
        [scratch((3 * D, CAP), F32), scratch((3 * D, CAP), F32)],
        lengths, got,
    )
    send, grad = call(
        bwd_kernel,
        (sds((TEAM, QB + LB * OB, CAP)), sds((CAP, D))),
        [
            scratch((D, CAP), F32),
            scratch((TEAM, OB, CAP), F32),
            scratch((TEAM, OB, CAP), F32),
            scratch((3 * D, CAP), F32),
            scratch((3 * D, CAP), F32),
        ],
        lengths, offsets, got, qkv_t, prob, context, out_mine, out_theirs, smem=2,
    )
    send, ctx_t = together(send, ctx_t)
    rows_x = scratch((NX, EX, D), BF)
    along = call(
        out_kernel,
        (sds((EX, D)),) * NX,
        [scratch((D, CAP), F32), scratch((TEAM, OB, CAP), F32), rows_x],
        lengths, offsets, tokens, ctx_t, out_mine, out_theirs, smem=2,
    )
    near = [a if step == 0 else to_right(a, step) for step, a in enumerate(along)]
    got, *near = together(exchange(send, team), *near)
    send = call(
        grads_kernel,
        sds((NY, EY + PIECE, D)),
        [scratch((QB, D), F32), scratch((OB, D), F32), scratch((PIECE, D), F32), rows_x],
        got, normed, *near, smem=0,
    )
    send, got = together(send, got)
    term, other = call(
        terms_kernel,
        (sds((NX, CAP, D)), sds((NX, CAP, D))),
        [], got, w_block, smem=0,
    )
    got = exchange(send, "y")
    own, right, across, left = call(
        pair_kernel, (sds((CAP, D)),) * NX, [], term, swap(other), smem=0
    )
    got, right, across, left = together(got, to_right(right, 1), across, left)
    terms = own, right, to_right(across, 2), to_right(left, NX - 1)
    embeds = call(place_kernel, sds((seq_rows, D)), [], offsets, got)
    total = jnp.sum(got[:, EY:].astype(F32), axis=0).astype(BF)
    got = exchange(jnp.broadcast_to(total[None], (NZ, PIECE, D)), "z")
    d_patches = call(
        patches_kernel, sds((CAP, D)), [],
        tokens, grad, *terms, smem=0,
    )
    got, d_patches, embeds = together(got, d_patches, embeds)
    factor = 1.0 / math.sqrt(CAP * OWNERS * 2 * NZ)
    own = jnp.sum(got.astype(F32), axis=0) * factor
    other = swap(own)
    grad_qkv, grad_out = call(
        join_kernel, (sds((2 * QP, D), F32), sds((2 * OP, D), F32)), [], own, other, smem=0
    )
    return embeds, d_patches.reshape(patches.shape), grad_qkv.T, grad_out.T


def solution(mesh):
    axes = Mesh(mesh.devices.reshape(NZ, 2, NY, NX), ("z", "core", "y", "x"))
    group, plane = ("z", "core"), ("y", "x")
    return jax.shard_map(
        local,
        mesh=axes,
        in_specs=(
            P(group + plane, None, None),
            P(group),
            P(group),
            P(None, plane),
            P(None, plane),
            P(group + plane, None),
        ),
        out_specs=(
            P(group + plane, None),
            P(group + plane, None, None),
            P(None, plane),
            P(None, plane),
        ),
        check_vma=False,
    )
```
